32 devices in a mesh: fsdp: 2 (over y), replica: 16 (over z, x, core).
Axes of the slice: x: 2, y: 2, z: 4, core: 2. Of those that a mesh axis runs over, the one named last changes fastest.
Arguments:
- inputs: bfloat16 [16, 1024, 960], P('replica', 'fsdp'), may hold values from -6 to 6
- segment_ids: int32 [16, 1024], P('replica'), may hold values from 0 to 1, as said below
- positions: int32 [16, 1024], P('replica', 'fsdp'), may hold values from 0 to 1023, as said below
- attn_gain: bfloat16 [960], P('fsdp'), may hold values from 0.099609375 to 1.8984375
- q_weight: bfloat16 [960, 960], P('fsdp'), may hold values from -0.25 to 0.25
- key_matrix: bfloat16 [320, 960], P('fsdp'), may hold values from -0.25 to 0.25
- value_matrix: bfloat16 [320, 960], P('fsdp'), may hold values from -0.1875 to 0.1875
- o_weight: bfloat16 [960, 960], P('fsdp'), may hold values from -1.5 to 1.5
- ffn_gain: bfloat16 [960], P('fsdp'), may hold values from 0.099609375 to 1.8984375
- gate_weight: bfloat16 [2560, 960], P('fsdp'), may hold values from -0.1875 to 0.1875
- up_weight: bfloat16 [2560, 960], P('fsdp'), may hold values from -0.1875 to 0.1875
- down_weight: bfloat16 [2560, 960], P('fsdp'), may hold values from -0.125 to 0.125
- cotangent: bfloat16 [16, 1024, 960], P('replica', 'fsdp'), may hold values from -6 to 6
Outputs:
- outputs: bfloat16 [16, 1024, 960], P('replica', 'fsdp')
- input_grad: float32 [16, 1024, 960], P('replica', 'fsdp')
- attn_gain_grad: float32 [960], P('fsdp')
- q_weight_grad: float32 [960, 960], P('fsdp')
- k_weight_grad: float32 [320, 960], P('fsdp')
- v_weight_grad: float32 [320, 960], P('fsdp')
- o_weight_grad: float32 [960, 960], P('fsdp')
- ffn_gain_grad: float32 [960], P('fsdp')
- gate_weight_grad: float32 [2560, 960], P('fsdp')
- up_weight_grad: float32 [2560, 960], P('fsdp')
- down_weight_grad: float32 [2560, 960], P('fsdp')
The draws below stay inside these ranges and needn't reach their ends.
Inputs may be any that keep to these rules, and one draw needn't show every extreme that they name: `segment_ids`: in each sequence the first h tokens have number 0 and the rest number 1, with h from 128 to 384. Within a document positions rise by one from token to token; the document numbered 1 starts at position 0.
All inputs are finite; a program needn't handle non-finite values.
Results may differ from the reference program's by a relative error of at most 0.023.
Values may be sent and summed in bfloat16 or wider, within the bound.
A program may use at most 256 MiB of HBM per device.

```python
import jax
import jax.numpy as jnp
from jax import lax

MODEL_WIDTH = 960
QUERY_HEADS = 15
KEY_VALUE_HEADS = 5
HEAD_SIZE = 64
FF = 2560
SEQ_LEN = 1024
TOK_DEV = 512
SEQS = 16


def head_counts(key):
    return jax.random.randint(key, (SEQS,), TOK_DEV // 4, 3 * TOK_DEV // 4 + 1)


def draw_segment_ids(key, part):
    counts = head_counts(key)
    index = jnp.arange(SEQ_LEN)
    return (index[None, :] >= counts[:, None]).astype(jnp.int32)


def draw_positions(key, part):
    counts = head_counts(key)
    key = jax.random.fold_in(key, 2)
    starts = jax.random.randint(key, (SEQS,), 0, SEQ_LEN - counts + 1)
    starts = jnp.where(jnp.arange(SEQS) == 0, SEQ_LEN - counts, starts)
    index = jnp.arange(SEQ_LEN)[None, :]
    head = starts[:, None] + index
    rest = index - counts[:, None]
    return jnp.where(index < counts[:, None], head, rest).astype(jnp.int32)


def level_of(own_key, shape, cuts, smallest, top_value):
    def one(position, blocks):
        heights = jax.random.uniform(jax.random.fold_in(jax.random.fold_in(own_key, 6), position), (blocks,), jnp.float32, smallest / len(cuts), top_value / len(cuts))
        return jnp.repeat(jnp.exp(heights), shape[position] // blocks).reshape((-1,) + (1,) * (len(shape) - position - 1))

    factor_of = one(*cuts[0])
    for cut in cuts[1:]:
        factor_of = factor_of * one(*cut)
    return factor_of


def centred(stream_key, shape, width, most, split=(), held_as=jnp.bfloat16):
    entries = width * jax.random.normal(stream_key, shape, jnp.float32)
    if split:
        entries = entries * level_of(stream_key, shape, split, -0.22, 0.18)
    return jnp.clip(entries, -most, most).astype(held_as)


def setup_inputs(seed: int = 0) -> dict:
    seeds = jax.random.split(jax.random.key(seed), 14)
    return {
        "inputs": centred(seeds[0], (SEQS, SEQ_LEN, MODEL_WIDTH), 1.0, 6.0, ((0, 16), (1, 2))),
        "segment_ids": draw_segment_ids(jax.random.fold_in(seeds[13], 71), 0),
        "positions": draw_positions(jax.random.fold_in(seeds[13], 71), 0),
        "attn_gain": jnp.clip(1.0 + 0.18 * jax.random.normal(seeds[3], (MODEL_WIDTH,), jnp.float32), 0.099609375, 1.8984375).astype(jnp.bfloat16),
        "q_weight": centred(seeds[4], (QUERY_HEADS * HEAD_SIZE, MODEL_WIDTH), (MODEL_WIDTH // 2) ** -0.5, 0.25, ((0, 2),)),
        "key_matrix": centred(seeds[5], (KEY_VALUE_HEADS * HEAD_SIZE, MODEL_WIDTH), (MODEL_WIDTH // 2) ** -0.5, 0.25, ((0, 2),)),
        "value_matrix": centred(seeds[6], (KEY_VALUE_HEADS * HEAD_SIZE, MODEL_WIDTH), MODEL_WIDTH ** -0.5, 0.1875, ((0, 2),)),
        "o_weight": centred(seeds[7], (MODEL_WIDTH, QUERY_HEADS * HEAD_SIZE), (max(QUERY_HEADS * HEAD_SIZE // 64, 4)) ** -0.5, 1.5, ((0, 2),)),
        "ffn_gain": jnp.clip(1.0 + 0.18 * jax.random.normal(seeds[8], (MODEL_WIDTH,), jnp.float32), 0.099609375, 1.8984375).astype(jnp.bfloat16),
        "gate_weight": centred(seeds[9], (FF, MODEL_WIDTH), MODEL_WIDTH ** -0.5, 0.1875, ((0, 2),)),
        "up_weight": centred(seeds[10], (FF, MODEL_WIDTH), MODEL_WIDTH ** -0.5, 0.1875, ((0, 2),)),
        "down_weight": centred(seeds[11], (FF, MODEL_WIDTH), FF ** -0.5, 0.125, ((0, 2),)),
        "cotangent": centred(seeds[12], (SEQS, SEQ_LEN, MODEL_WIDTH), 1.0, 6.0, ((0, 16), (1, 2))),
    }


@jax.custom_vjp
def lower_precision(v):
    return lax.optimization_barrier(v.astype(jnp.bfloat16)).astype(jnp.float32)

@jax.custom_vjp
def low_back(v):
    return v

def low_keep(v):
    return (lower_precision(v), None)

def low_pass(kept, grad):
    return (grad,)

def back_keep(v):
    return (v, None)

def back_low(kept, grad):
    return (lower_precision(grad),)
lower_precision.defvjp(low_keep, low_pass)
low_back.defvjp(back_keep, back_low)
norm_eps = 1e-05
rotary_base = 100000.0
highest_precision = lax.Precision.HIGHEST

def normalize(value_rows):
    return value_rows * lax.rsqrt(lax.optimization_barrier(jnp.mean(value_rows * value_rows, axis=-1, keepdims=True)) + norm_eps)

def project_rows(left, weight):
    return lax.dot_general(left, weight, (((1,), (1,)), ((), ())), precision=highest_precision)

def rotary_tables(positions):
    half = HEAD_SIZE // 2
    frequency = rotary_base ** (-(jnp.arange(half, dtype=jnp.float32) * 2.0 / HEAD_SIZE))
    angles = positions.astype(jnp.float32)[:, None] * frequency[None, :]
    cosine_table = jnp.concatenate([jnp.cos(angles), jnp.cos(angles)], axis=-1)[:, None, :]
    sine_table = jnp.concatenate([jnp.sin(angles), jnp.sin(angles)], axis=-1)[:, None, :]
    return (cosine_table, sine_table)

def apply_rotary(field, cosine_table, sine_table):
    half = HEAD_SIZE // 2
    turned = jnp.concatenate([-field[..., half:], field[..., :half]], axis=-1)
    return field * cosine_table + turned * sine_table

def sequence_layer(params, data, segments, positions):
    attn_gain, q_weight, key_matrix, value_matrix, o_weight, ffn_gain, gate_weight, up_weight, down_weight = params
    sequence_length = data.shape[0]
    head_group = QUERY_HEADS // KEY_VALUE_HEADS
    normed = normalize(data)
    hidden_state = lower_precision(normed * attn_gain)
    query_rows = low_back(project_rows(hidden_state, q_weight))
    key_rows = low_back(project_rows(hidden_state, key_matrix))
    value_rows = lower_precision(low_back(project_rows(hidden_state, value_matrix)))
    cosine_table, sine_table = rotary_tables(positions)
    query_rows = lower_precision(apply_rotary(query_rows.reshape(sequence_length, QUERY_HEADS, HEAD_SIZE), cosine_table, sine_table))
    key_rows = lower_precision(apply_rotary(key_rows.reshape(sequence_length, KEY_VALUE_HEADS, HEAD_SIZE), cosine_table, sine_table))
    grouped_heads = query_rows.reshape(sequence_length, KEY_VALUE_HEADS, head_group, HEAD_SIZE)
    scores = jnp.einsum('qkrd,skd->krqs', grouped_heads, key_rows, precision=highest_precision) * HEAD_SIZE ** (-0.5)
    scores = low_back(scores)
    index = jnp.arange(sequence_length)
    allowed = (segments[:, None] == segments[None, :]) & (index[:, None] >= index[None, :])
    scores = jnp.where(allowed[None, None], scores, -1e+30)
    top = lax.optimization_barrier(jnp.max(scores, axis=-1, keepdims=True))
    raised = jnp.exp(scores - top)
    attention_step = lower_precision(raised / lax.optimization_barrier(jnp.sum(raised, axis=-1, keepdims=True)))
    mixed_output = jnp.einsum('nluh,hng->unlg', attention_step, value_rows.reshape(sequence_length, KEY_VALUE_HEADS, HEAD_SIZE), precision=highest_precision)
    mixed_output = lower_precision(low_back(mixed_output.reshape(sequence_length, QUERY_HEADS * HEAD_SIZE)))
    middle = data + low_back(project_rows(mixed_output, o_weight))
    normed_two = normalize(middle)
    hidden_two = lower_precision(normed_two * ffn_gain)
    gate = low_back(project_rows(hidden_two, gate_weight))
    up = low_back(project_rows(hidden_two, up_weight))
    active = lower_precision(gate * jax.nn.sigmoid(gate) * up)
    down = low_back(jnp.dot(active, down_weight, precision=highest_precision))
    return middle + down

def reference(inputs, segment_ids, positions, attn_gain, q_weight, key_matrix, value_matrix, o_weight, ffn_gain, gate_weight, up_weight, down_weight, cotangent):
    params = tuple((weight.astype(jnp.float32) for weight in (attn_gain, q_weight, key_matrix, value_matrix, o_weight, ffn_gain, gate_weight, up_weight, down_weight)))

    def forward(params, data):

        def one_sequence(carry, item):
            return (carry, sequence_layer(params, item[0], item[1], item[2]))
        start = jnp.zeros((), jnp.float32)
        final, result = lax.scan(jax.checkpoint(one_sequence), start, (data, segment_ids, positions))
        return result
    result, pullback = jax.vjp(forward, params, inputs.astype(jnp.float32))
    param_back, input_back = pullback(cotangent.astype(jnp.float32))
    return (result.astype(jnp.bfloat16), input_back, param_back[0], param_back[1], param_back[2], param_back[3], param_back[4], param_back[5], param_back[6], param_back[7], param_back[8])
```

```python
import functools

import jax
import jax.numpy as jnp
from jax import lax
from jax.experimental import pallas as pl
from jax.experimental.pallas import tpu as pltpu
from jax.sharding import PartitionSpec as P

QUERY_HEADS = 15
KEY_VALUE_HEADS = 5
HEAD_SIZE = 64


norm_eps = 1e-05
rotary_base = 100000.0


def normalize_parts(value_rows):
    factor = lax.rsqrt(jnp.mean(value_rows * value_rows, axis=-1, keepdims=True) + norm_eps)
    return (value_rows * factor, factor)


def norm_back(upstream, normed, factor):
    return factor * (upstream - normed * jnp.mean(upstream * normed, axis=-1, keepdims=True))


def project_rows(left, weight):
    return lax.dot_general(
        left, weight, (((1,), (1,)), ((), ())), preferred_element_type=jnp.float32
    )


def contract_rows(left, right):
    return lax.dot_general(
        left, right, (((0,), (0,)), ((), ())), preferred_element_type=jnp.float32
    )


def swiglu_back(active_back, gate, up):
    sigma = jax.nn.sigmoid(gate)
    gate_back = (active_back * up * sigma * (1.0 + gate * (1.0 - sigma))).astype(jnp.bfloat16)
    up_back = (active_back * gate * sigma).astype(jnp.bfloat16)
    return (gate_back, up_back)


def dims(left, right, left_axis, right_axis):
    return lax.dot_general(
        left, right, (((left_axis,), (right_axis,)), ((), ())), preferred_element_type=jnp.float32
    )


def rotary_tables(positions):
    half = HEAD_SIZE // 2
    frequency = rotary_base ** (-(jnp.arange(half, dtype=jnp.float32) * 2.0 / HEAD_SIZE))
    angles = frequency[:, None] * positions.astype(jnp.float32)[None, :]
    cosine, sine = jnp.cos(angles), jnp.sin(angles)
    return (
        jnp.concatenate([cosine, cosine], axis=0)[None],
        jnp.concatenate([sine, sine], axis=0)[None],
    )


def apply_rotary(field, cosine_table, sine_table):
    half = HEAD_SIZE // 2
    turned = jnp.concatenate([-field[:, half:], field[:, :half]], axis=1)
    return field * cosine_table + turned * sine_table


def apply_rotary_back(field, cosine_table, sine_table):
    half = HEAD_SIZE // 2
    scaled = field * sine_table
    turned = jnp.concatenate([scaled[:, half:], -scaled[:, :half]], axis=1)
    return field * cosine_table + turned


def fill_bias(me_ref, segk_ref, segq_ref, bias_ref):
    @pl.when(pl.program_id(0) == 0)
    def _():
        keys, queries = bias_ref.shape
        key_index = lax.broadcasted_iota(jnp.int32, (keys, queries), 0)
        query_index = lax.broadcasted_iota(jnp.int32, (keys, queries), 1) + me_ref[0] * queries
        allowed = (segk_ref[...] == segq_ref[...]) & (key_index <= query_index)
        bias_ref[...] = jnp.where(allowed, 0.0, -1e30)


def attend_kernel(
    parts, block, me_ref, segk_ref, segq_ref, q_ref, k_ref, v_ref, o_ref, lse_ref, bias_ref
):
    fill_bias(me_ref, segk_ref, segq_ref, bias_ref)
    group, _, tokens = q_ref.shape

    for part in range(parts):

        @pl.when(me_ref[0] == part)
        def _():
            for start in range(0, tokens, block):
                span = part * tokens + start + block
                for head in range(group):
                    columns = slice(start, start + block)
                    scores = dims(k_ref[0, :, :span], q_ref[head, :, columns], 0, 0)
                    scores = scores + bias_ref[:span, columns]
                    top = jnp.max(scores, axis=0, keepdims=True)
                    raised = jnp.exp(scores - top)
                    total = jnp.sum(raised, axis=0, keepdims=True)
                    mixed = dims(v_ref[0, :, :span], raised.astype(jnp.bfloat16), 1, 0)
                    o_ref[head, :, columns] = (mixed / total).astype(jnp.bfloat16)
                    lse_ref[head, :, columns] = top + jnp.log(total)


def attend_back_kernel(
    parts,
    block,
    me_ref,
    segk_ref,
    segq_ref,
    q_ref,
    k_ref,
    v_ref,
    o_ref,
    lse_ref,
    do_ref,
    dq_ref,
    dk_ref,
    dv_ref,
    bias_ref,
):
    fill_bias(me_ref, segk_ref, segq_ref, bias_ref)
    group, _, tokens = q_ref.shape
    dk_ref[...] = jnp.zeros_like(dk_ref)
    dv_ref[...] = jnp.zeros_like(dv_ref)

    for part in range(parts):

        @pl.when(me_ref[0] == part)
        def _():
            for start in range(0, tokens, block):
                span = part * tokens + start + block
                for head in range(group):
                    columns = slice(start, start + block)
                    query = q_ref[head, :, columns]
                    back = do_ref[head, :, columns]
                    delta = jnp.sum(
                        back.astype(jnp.float32) * o_ref[head, :, columns].astype(jnp.float32),
                        axis=0,
                        keepdims=True,
                    )
                    scores = dims(k_ref[0, :, :span], query, 0, 0) + bias_ref[:span, columns]
                    attend = jnp.exp(scores - lse_ref[head, :, columns])
                    attend_back = dims(v_ref[0, :, :span], back, 0, 0)
                    score_back = (attend * (attend_back - delta)).astype(jnp.bfloat16)
                    dv_ref[0, :, :span] += dims(back, attend.astype(jnp.bfloat16), 1, 1)
                    dk_ref[0, :, :span] += dims(query, score_back, 1, 1)
                    dq_ref[head, :, columns] = dims(k_ref[0, :, :span], score_back, 1, 0)


def attention_specs(tokens, sequence):
    group = QUERY_HEADS // KEY_VALUE_HEADS
    return dict(
        me=pl.BlockSpec(memory_space=pltpu.SMEM),
        segk=pl.BlockSpec((sequence, 1), lambda h: (0, 0)),
        segq=pl.BlockSpec((1, tokens), lambda h: (0, 0)),
        query=pl.BlockSpec((group, HEAD_SIZE, tokens), lambda h: (h, 0, 0)),
        key=pl.BlockSpec((1, HEAD_SIZE, sequence), lambda h: (h, 0, 0)),
        row=pl.BlockSpec((group, 1, tokens), lambda h: (h, 0, 0)),
    )


def attend(parts, me, segk, segq, query, key, value):
    tokens, sequence = query.shape[2], key.shape[2]
    sp = attention_specs(tokens, sequence)
    pairs = QUERY_HEADS * tokens * sequence
    return pl.pallas_call(
        functools.partial(attend_kernel, parts, min(tokens, 256)),
        grid=(KEY_VALUE_HEADS,),
        in_specs=[sp["me"], sp["segk"], sp["segq"], sp["query"], sp["key"], sp["key"]],
        out_specs=[sp["query"], sp["row"]],
        out_shape=[
            jax.ShapeDtypeStruct(query.shape, jnp.bfloat16),
            jax.ShapeDtypeStruct((QUERY_HEADS, 1, tokens), jnp.float32),
        ],
        scratch_shapes=[pltpu.VMEM((sequence, tokens), jnp.float32)],
        compiler_params=pltpu.CompilerParams(vmem_limit_bytes=40 * 2**20),
        cost_estimate=pl.CostEstimate(
            flops=16 * HEAD_SIZE * pairs, bytes_accessed=4 * 2**20, transcendentals=pairs
        ),
    )(me, segk, segq, query, key, value)


def attend_grads(parts, me, segk, segq, query, key, value, mixed, lse, back):
    tokens, sequence = query.shape[2], key.shape[2]
    sp = attention_specs(tokens, sequence)
    pairs = QUERY_HEADS * tokens * sequence
    return pl.pallas_call(
        functools.partial(attend_back_kernel, parts, min(tokens, 256)),
        grid=(KEY_VALUE_HEADS,),
        in_specs=[sp["me"], sp["segk"], sp["segq"], sp["query"], sp["key"], sp["key"]]
        + [sp["query"], sp["row"], sp["query"]],
        out_specs=[sp["query"], sp["key"], sp["key"]],
        out_shape=[
            jax.ShapeDtypeStruct(query.shape, jnp.float32),
            jax.ShapeDtypeStruct(key.shape, jnp.float32),
            jax.ShapeDtypeStruct(key.shape, jnp.float32),
        ],
        scratch_shapes=[pltpu.VMEM((sequence, tokens), jnp.float32)],
        compiler_params=pltpu.CompilerParams(vmem_limit_bytes=48 * 2**20),
        cost_estimate=pl.CostEstimate(
            flops=40 * HEAD_SIZE * pairs, bytes_accessed=10 * 2**20, transcendentals=pairs
        ),
    )(me, segk, segq, query, key, value, mixed, lse, back)


def swap(block, axis, size, bit=0):
    return lax.ppermute(block, axis, [(i, i ^ (1 << bit)) for i in range(size)])


def place(mine, other, which):
    rows = mine.shape[0]
    both = jnp.zeros((2 * rows,) + mine.shape[1:], mine.dtype)
    both = lax.dynamic_update_slice_in_dim(both, mine, which * rows, 0)
    return lax.dynamic_update_slice_in_dim(both, other, (1 - which) * rows, 0)


def take(block, which):
    rows = block.shape[0] // 2
    return lax.dynamic_slice_in_dim(block, which * rows, rows)


def halve(block, axis, size, bit=0):
    which = (lax.axis_index(axis) >> bit) & 1
    return take(block, which) + swap(take(block, 1 - which), axis, size, bit)


def unhalve(block, axis, size, bit=0):
    which = (lax.axis_index(axis) >> bit) & 1
    return place(block, swap(block, axis, size, bit), which)


def gather_weight(weight, fsdp, replica):
    if fsdp != 2 or replica % 2 or weight.ndim == 1:
        return lax.all_gather(weight, "fsdp", axis=0, tiled=True)
    part = swap(take(weight, lax.axis_index("replica") & 1), "fsdp", fsdp)
    other = unhalve(part, "replica", replica)
    return place(weight, other, lax.axis_index("fsdp"))


def scatter_rows(block, fsdp):
    if fsdp != 2:
        return lax.psum_scatter(block, "fsdp", scatter_dimension=0, tiled=True)
    return halve(block, "fsdp", fsdp)


def replica_sum(block, replica):
    bits = replica.bit_length() - 1
    rows = block.shape[0]
    if replica != 1 << bits or rows % (2 * replica) or bits < 2:
        return lax.psum(block, "replica")
    block = halve(block, "replica", replica, 0)
    rows = block.shape[0] // 2
    orders = [list(range(1, bits)), list(range(1, bits))[::-1]]
    pieces = [block[:rows], block[rows:]]
    for step in range(bits - 1):
        pieces = [halve(p, "replica", replica, o[step]) for p, o in zip(pieces, orders)]
    for step in reversed(range(bits - 1)):
        pieces = [unhalve(p, "replica", replica, o[step]) for p, o in zip(pieces, orders)]
    return unhalve(jnp.concatenate(pieces), "replica", replica, 0)


def feed_forward(hidden, back, gate_weight, up_weight, down_weight):
    gate = project_rows(hidden, gate_weight)
    up = project_rows(hidden, up_weight)
    active = (gate * jax.nn.sigmoid(gate) * up).astype(jnp.bfloat16)
    gate_back, up_back = swiglu_back(project_rows(back, down_weight), gate, up)
    hidden_back = (
        jnp.dot(gate_back, gate_weight, preferred_element_type=jnp.float32)
        + jnp.dot(up_back, up_weight, preferred_element_type=jnp.float32)
    ).astype(jnp.bfloat16)
    down = jnp.dot(active, down_weight, preferred_element_type=jnp.float32).astype(jnp.bfloat16)
    return hidden_back, down, active, gate_back, up_back


def on_device(
    fsdp,
    replica,
    inputs,
    segment_ids,
    positions,
    attn_gain,
    q_weight,
    key_matrix,
    value_matrix,
    o_weight,
    ffn_gain,
    gate_weight,
    up_weight,
    down_weight,
    cotangent,
):
    tokens = inputs.shape[1]
    scale = HEAD_SIZE ** (-0.5)
    me = lax.axis_index("fsdp")
    me_ref = me.astype(jnp.int32)[None]
    data = inputs[0].astype(jnp.float32)
    segments = segment_ids[0]
    segk = segments[:, None]
    segq = lax.dynamic_slice_in_dim(segments, me * tokens, tokens)[None]
    cosine_table, sine_table = rotary_tables(positions[0])
    down_back = cotangent[0]
    back_out = down_back.astype(jnp.float32)

    kv_weight = jnp.concatenate([key_matrix, value_matrix])
    kv_rows = key_matrix.shape[0]
    gains = jnp.stack([attn_gain, ffn_gain], axis=1)
    gains = lax.all_gather(gains, "fsdp", axis=0, tiled=True) if fsdp != 2 else place(
        gains, swap(gains, "fsdp", fsdp), me
    )
    gain_first = gains[:, 0].astype(jnp.float32)
    gain_second = gains[:, 1].astype(jnp.float32)
    kv_gathered = gather_weight(kv_weight, fsdp, replica).reshape(fsdp, 2, kv_rows, -1)
    kv_full = jnp.swapaxes(kv_gathered, 0, 1).reshape(2 * fsdp * kv_rows, -1)
    q_weight, kv_full = lax.optimization_barrier((q_weight, kv_full))
    query_full = gather_weight(q_weight, fsdp, replica)

    normed, factor_one = normalize_parts(data)
    hidden_state = (normed * gain_first).astype(jnp.bfloat16)
    kv_lin = project_rows(kv_full, hidden_state).reshape(2 * KEY_VALUE_HEADS, HEAD_SIZE, tokens)
    kv_own = jnp.concatenate(
        [
            apply_rotary(kv_lin[:KEY_VALUE_HEADS], cosine_table, sine_table),
            kv_lin[KEY_VALUE_HEADS:],
        ]
    ).astype(jnp.bfloat16)
    if fsdp == 2:
        kv_first = lax.ppermute(kv_own, "fsdp", [(0, 1)])
        kv_all = jnp.concatenate([jnp.where(me == 0, kv_own, kv_first), kv_own], axis=2)
    else:
        kv_all = lax.all_gather(kv_own, "fsdp", axis=2, tiled=True)
    keys, values = kv_all[:KEY_VALUE_HEADS], kv_all[KEY_VALUE_HEADS:]
    o_weight, down_back_sent, kv_own = lax.optimization_barrier((o_weight, down_back, kv_own))
    out_full = gather_weight(o_weight, fsdp, replica)
    if fsdp == 2:
        back_other = swap(down_back_sent, "fsdp", fsdp)
    queries = (
        apply_rotary(
            project_rows(query_full, hidden_state).reshape(QUERY_HEADS, HEAD_SIZE, tokens),
            cosine_table,
            sine_table,
        ).astype(jnp.bfloat16)
        * scale
    ).astype(jnp.bfloat16)
    mixed, lse = attend(fsdp, me_ref, segk, segq, queries, keys, values)
    mixed_rows = mixed.reshape(QUERY_HEADS * HEAD_SIZE, tokens)
    middle = data + dims(mixed_rows, out_full, 0, 1)
    normed_two, factor_two = normalize_parts(middle)
    hidden_two = (normed_two * gain_second).astype(jnp.bfloat16)

    weights = (gate_weight, up_weight, down_weight)
    if fsdp == 2:
        hidden_other = swap(hidden_two, "fsdp", fsdp)
        own = feed_forward(hidden_two, down_back, *weights)
        hidden_other, own = lax.optimization_barrier((hidden_other, own))
        other = feed_forward(hidden_other, back_other, *weights)
        came_back = swap(other[0], "fsdp", fsdp)
        came_down = swap(other[1], "fsdp", fsdp)
        hidden_two_back = own[0].astype(jnp.float32) + came_back.astype(jnp.float32)
        down = own[1].astype(jnp.float32) + came_down.astype(jnp.float32)
        halves = ((own, hidden_two, down_back), (other, hidden_other, back_other))
        ffn_terms = (
            sum(contract_rows(w[3], h) for w, h, b in halves),
            sum(contract_rows(w[4], h) for w, h, b in halves),
            sum(contract_rows(w[2], b) for w, h, b in halves),
        )
    else:
        every_hidden = lax.all_gather(hidden_two, "fsdp", axis=0, tiled=True)
        every_back = lax.all_gather(down_back, "fsdp", axis=0, tiled=True)
        work = feed_forward(every_hidden, every_back, *weights)
        hidden_two_back = scatter_rows(work[0], fsdp).astype(jnp.float32)
        down = scatter_rows(work[1], fsdp).astype(jnp.float32)
        ffn_terms = (
            contract_rows(work[3], every_hidden),
            contract_rows(work[4], every_hidden),
            contract_rows(work[2], every_back),
        )
    outputs = (middle + down).astype(jnp.bfloat16)[None]
    ffn_sums = [lax.psum(t.astype(jnp.bfloat16), "replica").astype(jnp.float32) for t in ffn_terms]

    gain_second_term = jnp.sum(hidden_two_back * normed_two, axis=0)
    middle_back = back_out + norm_back(hidden_two_back * gain_second, normed_two, factor_two)
    attn_back = middle_back.astype(jnp.bfloat16)
    mixed_back = dims(out_full, attn_back, 0, 1).astype(jnp.bfloat16)
    out_term = dims(attn_back, mixed_rows, 0, 1).astype(jnp.bfloat16)
    query_rot_back, key_term, value_term = attend_grads(
        fsdp,
        me_ref,
        segk,
        segq,
        queries,
        keys,
        values,
        mixed,
        lse,
        mixed_back.reshape(mixed.shape),
    )
    kv_term = jnp.concatenate([key_term, value_term])
    if fsdp == 2:
        kv_sent = lax.ppermute(kv_term[:, :, :tokens].astype(jnp.bfloat16), "fsdp", [(1, 0)])
        kv_back = jnp.where(
            me == 0,
            kv_term[:, :, :tokens] + kv_sent.astype(jnp.float32),
            kv_term[:, :, tokens:],
        )
    else:
        kv_back = lax.psum_scatter(
            kv_term.astype(jnp.bfloat16), "fsdp", scatter_dimension=2, tiled=True
        ).astype(jnp.float32)
    query_back = (
        apply_rotary_back(query_rot_back * scale, cosine_table, sine_table)
        .reshape(QUERY_HEADS * HEAD_SIZE, tokens)
        .astype(jnp.bfloat16)
    )
    kv_back = jnp.concatenate(
        [
            apply_rotary_back(kv_back[:KEY_VALUE_HEADS], cosine_table, sine_table),
            kv_back[KEY_VALUE_HEADS:],
        ]
    )
    kv_back = kv_back.reshape(2 * KEY_VALUE_HEADS * HEAD_SIZE, tokens).astype(jnp.bfloat16)
    hidden_back = dims(query_back, query_full, 0, 0) + dims(kv_back, kv_full, 0, 0)
    gain_first_term = jnp.sum(hidden_back * normed, axis=0)
    input_back = middle_back + norm_back(hidden_back * gain_first, normed, factor_one)

    def by_owner(term):
        return term.astype(jnp.bfloat16).reshape(fsdp, -1, term.shape[-1])

    kv_grad = jnp.dot(kv_back, hidden_state, preferred_element_type=jnp.float32)
    key_grad, value_grad = jnp.split(kv_grad, 2)
    query_grad = jnp.dot(query_back, hidden_state, preferred_element_type=jnp.float32)
    width = hidden_state.shape[-1]
    gain_terms = jnp.stack([gain_first_term, gain_second_term]).reshape(2, fsdp, -1)
    gain_terms = jnp.swapaxes(gain_terms, 0, 1).reshape(fsdp, -1)
    q_rows = q_weight.shape[0]
    pieces = [by_owner(t) for t in (query_grad, key_grad, value_grad, out_term)]
    used = sum(p.shape[1] for p in pieces)
    extra = -(used + 1) % (2 * replica * 2) + 1
    gain_rows = jnp.zeros((fsdp, extra, width), jnp.bfloat16)
    gain_rows = gain_rows.at[:, 0, : gain_terms.shape[1]].set(gain_terms.astype(jnp.bfloat16))
    late = jnp.concatenate(pieces + [gain_rows], axis=1)
    late = scatter_rows(late.reshape(-1, width), fsdp)
    late = replica_sum(late, replica).astype(jnp.float32)
    ends = [q_rows, q_rows + kv_rows, q_rows + 2 * kv_rows, 2 * q_rows + 2 * kv_rows]
    query_sum, key_sum, value_sum, out_sum, rest = jnp.split(late, ends)
    gain_len = attn_gain.shape[0]
    return (
        outputs,
        input_back[None],
        rest[0, :gain_len],
        query_sum,
        key_sum,
        value_sum,
        out_sum,
        rest[0, gain_len : 2 * gain_len],
        *ffn_sums,
    )


def solution(mesh):
    in_specs = (
        P("replica", "fsdp", None),
        P("replica", None),
        P("replica", "fsdp"),
        P("fsdp"),
        P("fsdp", None),
        P("fsdp", None),
        P("fsdp", None),
        P("fsdp", None),
        P("fsdp"),
        P("fsdp", None),
        P("fsdp", None),
        P("fsdp", None),
        P("replica", "fsdp", None),
    )
    out_specs = (
        P("replica", "fsdp", None),
        P("replica", "fsdp", None),
        P("fsdp"),
        P("fsdp", None),
        P("fsdp", None),
        P("fsdp", None),
        P("fsdp", None),
        P("fsdp"),
        P("fsdp", None),
        P("fsdp", None),
        P("fsdp", None),
    )
    return jax.shard_map(
        functools.partial(on_device, mesh.shape["fsdp"], mesh.shape["replica"]),
        mesh=mesh, in_specs=in_specs, out_specs=out_specs, check_vma=False
    )
```
